128 devices in a mesh: dp: 4 (over z), expert: 32 (over y, x, core).
Axes of the slice: x: 4, y: 4, z: 4, core: 2. Of those that a mesh axis runs over, the one named last changes fastest.
Arguments:
- table_rows: bfloat16 [8192, 2048], P('expert'), may hold values from -4 to 4
- item_owner: int32 [32768, 3, 1], P(('dp', 'expert')), may hold values from 0 to 31; in each aligned block of 768 rows (0 to 767, 768 to 1535, ..., all dimensions but the last counted through in order) at most 48 rows name the same one
- item_row: int32 [32768, 3], P(('dp', 'expert')), may hold values from 0 to 255
- norm_gain: float32 [2048], replicated, may hold values from 0.1 to 1.9
- router: bfloat16 [2048, 64], replicated, may hold values from -0.125 to 0.125
- w_gate: bfloat16 [64, 2048, 768], P('expert'), may hold values from -0.125 to 0.125
- w_up: bfloat16 [64, 2048, 768], P('expert'), may hold values from -0.125 to 0.125
- w_down: bfloat16 [64, 2048, 768], P('expert'), may hold values from -0.21875 to 0.21875
- experts_of: int32 [32768, 2], P(('dp', 'expert')), may hold values from 0 to 63, all different within a row; in each aligned block of 256 rows (0 to 255, 256 to 511, ...) at most 16 rows name the same one
- grad_mixed: bfloat16 [32768, 2048], P(('dp', 'expert')), may hold values from -6 to 6
Outputs:
- mixed: bfloat16 [32768, 2048], P(('dp', 'expert'))
- grad_w_gate: bfloat16 [64, 2048, 768], P('expert', 'dp')
- grad_w_up: bfloat16 [64, 2048, 768], P('expert', 'dp')
- grad_w_down: bfloat16 [64, 2048, 768], P('expert', 'dp')
The draws below stay inside these ranges and needn't reach their ends.
Inputs may be any that keep to these rules, and one draw needn't show every extreme that they name: `item_owner`: within the 256 x 3 lookups of one device, at most 48 name rows of one owner; on some device some owner is named exactly 48 times. `experts_of`: each event names 2 different experts. Within the 256 events of one device at most 16 name one expert; on some device some expert is named exactly 16 times.
All inputs are finite; a program needn't handle non-finite values.
Results may differ from the reference program's by a relative error of at most 0.02.
Values may be sent and summed in bfloat16 or wider, within the bound.
No kernel may reach another device: no remote copies, remote signals or barrier semaphores. Data moves between devices by JAX's collectives and lax.ppermute only.
A program may use at most 256 MiB of HBM per device.

```python
import math
import jax
import jax.numpy as jnp
import numpy as np
from jax import lax

D = 2048
FF = 768
TOP = 2
LEVELS = 3
TOK_DEV = 256
R_DEV = 256
OWNERS = 32
EXPERTS = 64
TOKENS = 32768
GROUP_TOK = 8192
CAP = 16
CAPF = 48
N_DP = 4


def plant(array, stream_key, low, largest):
    dims = array.shape
    spot = [jax.random.randint(jax.random.fold_in(stream_key, axis), (), 0, dims[axis]) for axis in range(len(dims))]
    array = array.at[tuple(spot)].set(low)
    longest = dims.index(max(dims))
    spot[longest] = (spot[longest] + 1) % dims[longest]
    return array.at[tuple(spot)].set(largest)


def block_levels(stream_key, shape, split, low, high):
    level = 1.0
    for dim, blocks in split:
        heights = jax.random.uniform(jax.random.fold_in(jax.random.fold_in(stream_key, 6), dim), (blocks,), jnp.float32, low / len(split), high / len(split))
        level = level * jnp.repeat(jnp.exp(heights), shape[dim] // blocks).reshape((-1,) + (1,) * (len(shape) - 1 - dim))
    return level


def shared_out(own_key, own, number, rows, number_of, top, bound, lean):
    ranking = jax.random.permutation(own_key, number_of)
    crowded, usual = load_shares(number_of, rows * top, bound, lean, True), load_shares(number_of, rows * top, bound, lean, False)
    places = jnp.arange(number_of)

    def named(lengths, turn):
        used = int((lengths > 0).sum())
        fixed = max(1, used // 4)
        passed = fixed + (places - fixed + turn * (used - fixed)) % max(1, number_of - fixed)
        return jnp.zeros((number_of,), jnp.int32).at[ranking[jnp.where(places < fixed, places, passed)]].set(jnp.asarray(lengths, jnp.int32))

    lengths = jnp.where(number % 4 == 0, named(crowded, number // 4), named(usual, number - number // 4 - 1))
    mixed = jax.random.permutation(jax.random.fold_in(own, 3), number_of)
    donor, receiver = mixed[0:number_of // 2 * 2:2], mixed[1:number_of // 2 * 2:2]
    room = jnp.minimum(lengths[donor] - 1, bound - lengths[receiver]) // 2
    room = jnp.where((donor == ranking[0]) | (receiver == ranking[0]) | (lengths[receiver] == 0), 0, jnp.maximum(room, 0))
    passed = jax.random.randint(jax.random.fold_in(own, 4), (number_of // 2,), 0, 1 << 20) % (room + 1)
    lengths = lengths.at[donor].add(-passed).at[receiver].add(passed)
    labels = jnp.searchsorted(jnp.cumsum(lengths), jnp.arange(rows * top), side="right").astype(jnp.int32)
    listing = labels.reshape(top, rows).T
    listing = listing[jax.random.permutation(jax.random.fold_in(own, 1), rows)]
    turn = jax.random.randint(jax.random.fold_in(own, 2), (rows, 1), 0, top)
    return jnp.take_along_axis(listing, (jnp.arange(top)[None, :] + turn) % top, axis=1)


def load_shares(count, total, reach, slope, full):
    portions = [(1 << 20) // math.isqrt(standing ** slope) + 1 for standing in range(1, count + 1)]
    largest = reach if full else min(reach, max(-(-total // count), total * portions[0] // sum(portions)))
    least = 1 if total - largest >= count - 1 else 0
    given, spare = [largest] + [least] * (count - 1), total - largest - least * (count - 1)
    while spare > 0:
        movable = [i for i in range(1, count) if given[i] < largest] or [i for i in range(1, count) if given[i] < reach]
        pool, budget = sum([portions[i] for i in movable]), spare
        for i in movable:
            extra = min(reach - given[i], max(1, budget * portions[i] // pool), spare)
            given[i] = given[i] + extra
            spare = spare - extra
    return np.array(given)


def normal_values(own_key, extent, deviation, bound, split=(), held_as=jnp.bfloat16):
    entries = deviation * jax.random.normal(own_key, extent, jnp.float32)
    if split:
        entries = entries * block_levels(own_key, extent, split, -0.22, 0.18)
    return jnp.clip(entries, -bound, bound).astype(held_as)


def setup_inputs(seed: int = 0) -> dict:
    seeds = jax.random.split(jax.random.key(seed), 11)
    table_rows = normal_values(seeds[0], (OWNERS * R_DEV, D), 0.6, 4.0, ((0, 32),))
    item_owner_keys = jax.random.split(jax.random.fold_in(seeds[1], 1), TOKENS * LEVELS // (TOK_DEV * LEVELS))
    item_owner_turns = jax.random.permutation(jax.random.fold_in(seeds[1], 3), TOKENS * LEVELS // (TOK_DEV * LEVELS))
    item_owner = jax.vmap(lambda own, number: shared_out(jax.random.fold_in(seeds[1], 2), own, number, TOK_DEV * LEVELS, OWNERS, 1, CAPF, 2))(item_owner_keys, item_owner_turns).reshape((TOKENS, LEVELS, 1))
    item_row = plant(jax.random.randint(seeds[2], (TOKENS, LEVELS), 0, R_DEV), jax.random.fold_in(seeds[2], 1), 0, R_DEV - 1).astype(jnp.int32)
    norm_gain = jnp.clip(1.0 + 0.18 * jax.random.normal(seeds[3], (D,), jnp.float32), 0.1, 1.9)
    router = normal_values(seeds[4], (D, EXPERTS), D ** -0.5, 0.125)
    w_gate = normal_values(seeds[5], (EXPERTS, D, FF), D ** -0.5, 0.125, ((0, 32),))
    w_up = normal_values(seeds[6], (EXPERTS, D, FF), D ** -0.5, 0.125, ((0, 32),))
    w_down = normal_values(seeds[7], (EXPERTS, D, FF), FF ** -0.5, 0.21875, ((0, 32),))
    experts_of_keys = jax.random.split(jax.random.fold_in(seeds[8], 1), TOKENS // TOK_DEV)
    experts_of_turns = jax.random.permutation(jax.random.fold_in(seeds[8], 3), TOKENS // TOK_DEV)
    experts_of = jax.vmap(lambda own, number: shared_out(jax.random.fold_in(seeds[8], 2), own, number, TOK_DEV, EXPERTS, TOP, CAP, 2))(experts_of_keys, experts_of_turns).reshape((TOKENS, TOP))
    grad_mixed = normal_values(seeds[9], (TOKENS, D), 1.0, 6.0, ((0, 128),))
    return {"table_rows": table_rows, "item_owner": item_owner, "item_row": item_row, "norm_gain": norm_gain, "router": router, "w_gate": w_gate, "w_up": w_up, "w_down": w_down, "experts_of": experts_of, "grad_mixed": grad_mixed}


def reference(table_rows, item_owner, item_row, norm_gain, router, w_gate, w_up, w_down, experts_of, grad_mixed):
    rows = (item_owner[:, :, 0] * R_DEV + item_row).astype(jnp.int32)
    summed = jnp.zeros((TOKENS, D), jnp.float32)
    for level in range(LEVELS):
        summed = summed + table_rows[rows[:, level]].astype(jnp.float32)
    embedded = summed.astype(jnp.bfloat16)
    base = lax.optimization_barrier(embedded).astype(jnp.float32)
    normed = (base * lax.rsqrt(lax.optimization_barrier(jnp.mean(base * base, axis=-1, keepdims=True)) + 1e-05) * norm_gain).astype(jnp.bfloat16)
    scores = jax.nn.sigmoid(jnp.dot(normed, router, preferred_element_type=jnp.float32))
    picked = jnp.take_along_axis(scores, experts_of, axis=1)
    weight = picked / lax.optimization_barrier(jnp.sum(picked, axis=1, keepdims=True))
    scaled = (weight[:, :, None] * grad_mixed.astype(jnp.float32)[:, None, :]).astype(jnp.bfloat16)
    pairs = TOKENS * TOP
    scaled_flat = scaled.reshape(pairs, D)
    weight_flat = weight.reshape(pairs)
    pair_ids = jnp.arange(pairs, dtype=jnp.int32)
    group = pair_ids // TOP // GROUP_TOK
    keys = (experts_of.reshape(pairs) * N_DP + group).astype(jnp.int32)
    order = jnp.argsort(keys, stable=True).astype(jnp.int32)
    counts = jax.ops.segment_sum(jnp.ones((pairs,), jnp.int32), keys, num_segments=EXPERTS * N_DP).astype(jnp.int32)
    starts = (jnp.cumsum(counts) - counts).astype(jnp.int32)
    block = OWNERS * CAP
    order_pad = jnp.concatenate([order, jnp.zeros((block,), jnp.int32)])
    positions = jnp.arange(block, dtype=jnp.int32)
    high = lax.Precision.HIGHEST

    def per_expert(acc, items):
        wg, wu, wd, expert = items
        wgf = wg.astype(jnp.float32)
        wuf = wu.astype(jnp.float32)
        wdf = wd.astype(jnp.float32)
        totals = [jnp.zeros((D, FF), jnp.float32) for _ in range(3)]
        for group_id in range(N_DP):
            slot_key = expert * N_DP + group_id
            index = lax.dynamic_slice(order_pad, (starts[slot_key].astype(jnp.int32),), (block,))
            valid = (positions < counts[slot_key]).astype(jnp.float32)[:, None]
            token = index // TOP
            rows_in = normed[token].astype(jnp.float32) * valid
            grads_in = scaled_flat[index].astype(jnp.float32) * valid
            gate = jnp.dot(rows_in, wgf, precision=high)
            up = jnp.dot(rows_in, wuf, precision=high)
            hidden = (jax.nn.silu(gate) * up).astype(jnp.bfloat16)
            hidden_f = lax.optimization_barrier(hidden).astype(jnp.float32)
            produced = jnp.dot(hidden_f, wdf.T, precision=high).astype(jnp.bfloat16)
            produced_f = lax.optimization_barrier(produced).astype(jnp.float32)
            acc = acc.at[token].add(weight_flat[index][:, None] * valid * produced_f)
            grad_hidden = jnp.dot(grads_in, wdf, precision=high)
            sig = jax.nn.sigmoid(gate)
            grad_gate = (grad_hidden * up * sig * (1.0 + gate * (1.0 - sig))).astype(jnp.bfloat16)
            grad_up = (grad_hidden * gate * sig).astype(jnp.bfloat16)
            part_gate = jnp.dot(rows_in.T, lax.optimization_barrier(grad_gate).astype(jnp.float32), precision=high)
            part_up = jnp.dot(rows_in.T, lax.optimization_barrier(grad_up).astype(jnp.float32), precision=high)
            part_down = jnp.dot(grads_in.T, hidden_f, precision=high)
            parts = [part_gate, part_up, part_down]
            for which in range(3):
                rounded = lax.optimization_barrier(parts[which].astype(jnp.bfloat16))
                totals[which] = totals[which] + rounded.astype(jnp.float32)
        return (acc, (totals[0].astype(jnp.bfloat16), totals[1].astype(jnp.bfloat16), totals[2].astype(jnp.bfloat16)))
    acc, grads = lax.scan(per_expert, jnp.zeros((TOKENS, D), jnp.float32), (w_gate, w_up, w_down, jnp.arange(EXPERTS, dtype=jnp.int32)))
    mixed = (base + acc).astype(jnp.bfloat16)
    return (mixed, grads[0], grads[1], grads[2])
```

```python
import functools

import jax
import jax.numpy as jnp
from jax import lax
from jax.experimental import pallas as pl
from jax.experimental.pallas import tpu as pltpu
from jax.sharding import PartitionSpec as P

BF16, F32, I32 = jnp.bfloat16, jnp.float32, jnp.int32
SIDE = 4
VMEM_BYTES = 56 * 1024 * 1024
PARAMS = pltpu.CompilerParams(vmem_limit_bytes=VMEM_BYTES)
WHOLE = pl.BlockSpec(memory_space=pltpu.VMEM)
SCALAR = pl.BlockSpec(memory_space=pltpu.SMEM)


def cost(flops, nbytes):
    return pl.CostEstimate(flops=int(flops), bytes_accessed=int(nbytes), transcendentals=0)


def dot(a, b):
    return lax.dot_general(a, b, (((1,), (0,)), ((), ())), preferred_element_type=F32)


def dot_t0(a, b):
    return lax.dot_general(a, b, (((0,), (0,)), ((), ())), preferred_element_type=F32)


def dot_t1(a, b):
    return lax.dot_general(a, b, (((1,), (1,)), ((), ())), preferred_element_type=F32)


def plane_perm(dy, dx, swap=0):
    pairs = []
    for y in range(SIDE):
        for x in range(SIDE):
            for c in range(2):
                to = ((y + dy) % SIDE) * SIDE + (x + dx) % SIDE
                pairs.append(((y * SIDE + x) * 2 + c, to * 2 + (c ^ swap)))
    return pairs


def send_plane(v, dy, dx):
    return lax.ppermute(v, "expert", plane_perm(dy, dx))


def send_sibling(v):
    return lax.ppermute(v, "expert", plane_perm(0, 0, 1))


def send_dp(v, step):
    return lax.ppermute(v, "dp", [(i, (i + step) % SIDE) for i in range(SIDE)])


def ring_pieces(a, dy, dx):
    half = a.shape[0] // 2
    before = send_plane(a, dy, dx)
    after = send_plane(a, -dy, -dx)
    opposite_low = send_plane(before[:half], dy, dx)
    opposite_high = send_plane(after[half:], -dy, -dx)
    return [a, before, after, opposite_low, opposite_high]


def route_kernel(exp_local, capacity, experts_ref, grad_ref, place_ref, *out_refs):
    tokens, top = experts_ref.shape
    owners_slots = place_ref.shape[1] // exp_local
    lanes = out_refs[0].shape[1] - grad_ref.shape[1]
    chosen = experts_ref[...]
    ids = lax.broadcasted_iota(I32, (tokens, lanes), 1)
    picks = [(chosen[:, k : k + 1] == ids).astype(F32) for k in range(top)]
    earlier = (
        lax.broadcasted_iota(I32, (tokens, tokens), 0)
        > lax.broadcasted_iota(I32, (tokens, tokens), 1)
    ).astype(F32).astype(BF16)
    slots = lax.broadcasted_iota(I32, (tokens, place_ref.shape[1]), 1)
    total = jnp.zeros((1, lanes), F32)
    hits = []
    for k in range(top):
        ahead = dot(earlier, picks[k].astype(BF16)) + total
        total = total + jnp.sum(picks[k], axis=0, keepdims=True)
        position = jnp.sum(ahead * picks[k], axis=1, keepdims=True).astype(I32)
        expert = chosen[:, k : k + 1]
        column = (
            lax.rem(expert, exp_local) * owners_slots
            + lax.div(expert, exp_local) * capacity
            + position
        )
        hits.append((slots == column).astype(F32))
    place_ref[...] = (hits[0] + hits[1]).astype(BF16)
    width = grad_ref.shape[1]
    for j in range(exp_local):
        span = slice(j * owners_slots, (j + 1) * owners_slots)
        place = (hits[0][:, span] + hits[1][:, span]).astype(BF16)
        for at in range(0, width, 512):
            out_refs[j][:, at : at + 512] = dot_t0(place, grad_ref[:, at : at + 512]).astype(BF16)
        partner = dot_t0(hits[0][:, span].astype(BF16), picks[1].astype(BF16)) + dot_t0(
            hits[1][:, span].astype(BF16), picks[0].astype(BF16)
        )
        out_refs[j][:, width:] = partner.astype(BF16)


def route(experts_of, grads, owners, exp_local, capacity):
    tokens, width = grads.shape
    slots = owners * capacity
    sent = jax.ShapeDtypeStruct((slots, width + 128), BF16)
    return pl.pallas_call(
        functools.partial(route_kernel, exp_local, capacity),
        out_shape=[jax.ShapeDtypeStruct((tokens, exp_local * slots), BF16)] + [sent] * exp_local,
        in_specs=[WHOLE, WHOLE],
        out_specs=[WHOLE] * (1 + exp_local),
        compiler_params=PARAMS,
        cost_estimate=cost(2 * tokens * exp_local * slots * width, 6e6),
        name="route",
    )(experts_of, grads)


def lookup_kernel(count, first, has_partial, *refs):
    pieces, rows_ref = refs[:count], refs[count]
    rest = refs[count + 1 :]
    wanted = rows_ref[...]
    levels = wanted.shape[1]
    if has_partial:
        total = rest[0][...]
        rest = rest[1:]
    else:
        total = jnp.zeros((wanted.shape[0], pieces[0].shape[1]), F32)
    at = first
    for piece in pieces:
        span = piece.shape[0]
        ids = lax.broadcasted_iota(I32, (wanted.shape[0], span), 1) + at
        many = (wanted[:, 0:1] == ids).astype(F32)
        for level in range(1, levels):
            many = many + (wanted[:, level : level + 1] == ids).astype(F32)
        total = total + dot(many.astype(BF16), piece[...])
        at += span
    if has_partial:
        block = pl.program_id(0)
        for i, out in enumerate(rest):

            @pl.when(block == i)
            def _():
                out[...] = total.astype(BF16)
    else:
        rest[0][...] = total


def lookup(pieces, rows, first, tok, partial=None):
    width = pieces[0].shape[1]
    tokens, levels = rows.shape
    blocks = tokens // tok
    held = sum(p.shape[0] for p in pieces)
    in_specs = [pl.BlockSpec(p.shape, lambda i: (0, 0)) for p in pieces]
    in_specs.append(pl.BlockSpec((tok, levels), lambda i: (i, 0)))
    args = list(pieces) + [rows]
    if partial is None:
        out_shape = jax.ShapeDtypeStruct((tokens, width), F32)
        out_specs = pl.BlockSpec((tok, width), lambda i: (i, 0))
    else:
        in_specs.append(pl.BlockSpec((tok, width), lambda i: (i, 0)))
        args.append(partial)
        out_shape = [jax.ShapeDtypeStruct((tok, width), BF16)] * blocks
        out_specs = [pl.BlockSpec((tok, width), lambda i: (0, 0))] * blocks
    return pl.pallas_call(
        functools.partial(lookup_kernel, len(pieces), first, partial is not None),
        grid=(blocks,),
        out_shape=out_shape,
        in_specs=in_specs,
        out_specs=out_specs,
        compiler_params=PARAMS,
        cost_estimate=cost(2 * tokens * held * width, held * width * 2 + tokens * width * 4),
        name="lookup",
    )(*args)


def dispatch_kernel(z_ref, gain_ref, place_ref, *refs):
    quarters, outs = refs[:SIDE], refs[SIDE:]
    cols = quarters[0].shape[1]
    base = [q[...].astype(F32) for q in quarters]
    total = sum(jnp.sum(b * b, axis=1, keepdims=True) for b in base)
    scale = lax.rsqrt(total / (SIDE * cols) + 1e-05)
    slots = outs[0].shape[0]
    for r in range(SIDE):
        at = pl.multiple_of(lax.rem(z_ref[0] + r, SIDE) * cols, cols)
        normed = (base[r] * scale * gain_ref[:, pl.ds(at, cols)]).astype(BF16)
        for j, out in enumerate(outs):
            place = place_ref[:, j * slots : (j + 1) * slots]
            out[:, pl.ds(at, cols)] = dot_t0(place, normed).astype(BF16)


def dispatch(z, gain, place, quarters, exp_local):
    tokens, cols = quarters[0].shape
    slots = place.shape[1] // exp_local
    return pl.pallas_call(
        dispatch_kernel,
        out_shape=[jax.ShapeDtypeStruct((slots, SIDE * cols), BF16)] * exp_local,
        in_specs=[SCALAR] + [WHOLE] * (2 + SIDE),
        out_specs=[WHOLE] * exp_local,
        compiler_params=PARAMS,
        cost_estimate=cost(2 * tokens * exp_local * slots * cols * SIDE, 6e6),
        name="dispatch",
    )(z, gain, place, *quarters)


def expert_kernel(
    ids_ref, x_ref, g_ref, router_ref, wg_ref, wu_ref, wd_ref, out_ref, *refs
):
    parts, (weight_ref, xt_ref, gt_ref, acc_ref) = refs[:8], refs[8:]
    step = pl.program_id(0)
    width = x_ref.shape[1]
    quarter = width // SIDE
    half = quarter // 2

    @pl.when(step == 0)
    def _():
        score = jax.nn.sigmoid(dot(x_ref[...], router_ref[...]))
        count = score.shape[1]
        lane = lax.broadcasted_iota(I32, score.shape, 1)
        own = jnp.sum(jnp.where(lane == ids_ref[1], score, 0.0), axis=1, keepdims=True)
        partner = g_ref[:, width : width + count].astype(F32)
        other = jnp.sum(score * partner, axis=1, keepdims=True)
        weight_ref[...] = own / (own + other)
        for at in range(0, width, quarter):
            xt_ref[at : at + quarter, :] = x_ref[:, at : at + quarter].T
            gt_ref[at : at + quarter, :] = g_ref[:, at : at + quarter].T
        acc_ref[...] = jnp.zeros_like(acc_ref)

    weight = weight_ref[...]
    gate = dot(x_ref[...], wg_ref[0])
    up = dot(x_ref[...], wu_ref[0])
    grad_hidden = dot(g_ref[:, :width], wd_ref[0]) * weight
    sig = jax.nn.sigmoid(gate)
    act = gate * sig
    hidden = (act * up * weight).astype(BF16)
    grad_gate = (grad_hidden * up * sig * (1.0 + gate * (1.0 - sig))).astype(BF16)
    grad_up = (grad_hidden * act).astype(BF16)
    acc_ref[...] += dot_t1(hidden, wd_ref[0])
    for r in range(SIDE):
        start = lax.rem(ids_ref[0] + r, SIDE) * quarter
        for h in range(2):
            rows = pl.ds(pl.multiple_of(start + h * half, half), half)
            part = parts[2 * r + h]
            part[0] = dot(xt_ref[rows, :], grad_gate).astype(BF16)
            part[1] = dot(xt_ref[rows, :], grad_up).astype(BF16)
            part[2] = dot(gt_ref[rows, :], hidden).astype(BF16)

    @pl.when(step == pl.num_programs(0) - 1)
    def _():
        out_ref[...] = acc_ref[...].astype(BF16)


def expert(ids, x, g, router, w_gate, w_up, w_down, j):
    slots, width = x.shape
    ff = w_gate.shape[2]
    chunk = 256 if ff % 256 == 0 else ff
    eighth = width // SIDE // 2
    held = pl.BlockSpec((1, width, chunk), lambda f, ids: (j, 0, f))
    fixed = lambda a: pl.BlockSpec(a.shape, lambda f, ids: (0, 0))
    part = jax.ShapeDtypeStruct((3, eighth, ff), BF16)
    grid_spec = pltpu.PrefetchScalarGridSpec(
        num_scalar_prefetch=1,
        grid=(ff // chunk,),
        in_specs=[fixed(x), fixed(g), fixed(router), held, held, held],
        out_specs=[pl.BlockSpec((slots, width), lambda f, ids: (0, 0))]
        + [pl.BlockSpec((3, eighth, chunk), lambda f, ids: (0, 0, f))] * 8,
        scratch_shapes=[
            pltpu.VMEM((slots, 1), F32),
            pltpu.VMEM((width, slots), BF16),
            pltpu.VMEM((width, slots), BF16),
            pltpu.VMEM((slots, width), F32),
        ],
    )
    return pl.pallas_call(
        expert_kernel,
        grid_spec=grid_spec,
        out_shape=[jax.ShapeDtypeStruct((slots, width), BF16)] + [part] * 8,
        compiler_params=PARAMS,
        cost_estimate=cost(14 * slots * width * ff, 12 * width * ff + 6 * slots * width),
        name="expert",
    )(ids, x, g, router, w_gate, w_up, w_down)


def finish_kernel(*refs):
    mine, before, after, outs = refs[0:2], refs[2:4], refs[4:6], refs[-3:]
    half = mine[0].shape[1]
    for h in range(2):
        for i in range(3):
            total = mine[h][i].astype(F32) + before[h][i].astype(F32) + after[h][i].astype(F32)
            outs[i][0, h * half : (h + 1) * half, :] = total.astype(BF16)


def finish(mine, before, after, j, exp_local, held=None):
    _, half, ff = mine[0].shape
    chunk = 256 if ff % 256 == 0 else ff
    block = pl.BlockSpec((3, half, chunk), lambda f: (0, 0, f))
    in_specs = [block] * 6
    args = [*mine, *before, *after]
    alias = {}
    if held is not None:
        in_specs += [pl.BlockSpec(memory_space=pl.ANY)] * 3
        args += list(held)
        alias = {6: 0, 7: 1, 8: 2}
    return pl.pallas_call(
        finish_kernel,
        grid=(ff // chunk,),
        out_shape=[jax.ShapeDtypeStruct((exp_local, 2 * half, ff), BF16)] * 3,
        in_specs=in_specs,
        out_specs=[pl.BlockSpec((1, 2 * half, chunk), lambda f: (j, 0, f))] * 3,
        input_output_aliases=alias,
        compiler_params=PARAMS,
        cost_estimate=cost(6 * half * ff * 3, 48 * half * ff),
        name="finish",
    )(*args)


def combine_kernel(z_ref, place_ref, *refs):
    quarters, backs, out = refs[:SIDE], refs[SIDE:-1], refs[-1]
    cols = quarters[0].shape[1]
    slots = backs[0].shape[0]
    for r in range(SIDE):
        at = pl.multiple_of(lax.rem(z_ref[0] + r, SIDE) * cols, cols)
        total = quarters[r][...].astype(F32)
        for j, back in enumerate(backs):
            total = total + dot(place_ref[:, j * slots : (j + 1) * slots], back[:, pl.ds(at, cols)])
        out[:, pl.ds(at, cols)] = total.astype(BF16)


def combine(z, place, quarters, backs):
    tokens, cols = quarters[0].shape
    return pl.pallas_call(
        combine_kernel,
        out_shape=jax.ShapeDtypeStruct((tokens, SIDE * cols), BF16),
        in_specs=[SCALAR] + [WHOLE] * (1 + SIDE + len(backs)),
        out_specs=WHOLE,
        compiler_params=PARAMS,
        cost_estimate=cost(2 * tokens * place.shape[1] * cols * SIDE, 7e6),
        name="combine",
    )(z, place, *quarters, *backs)


def row_places(owner, row, me, owner_rows):
    chip, core = owner // 2, owner % 2
    order = lambda d: jnp.where(d == 0, 0, jnp.where(d == 1, 2, jnp.where(d == 2, 3, 1)))
    dy = order((chip // SIDE - me // (2 * SIDE)) % SIDE)
    dx = order((chip % SIDE - (me // 2) % SIDE) % SIDE)
    half = owner_rows // 2
    inner = jnp.where(row < half, dy * SIDE + dx, dx * SIDE + dy) * half + row % half
    half_rows = SIDE * SIDE * half
    other = (core != me % 2).astype(I32)
    return other * (2 * half_rows) + jnp.where(row < half, 0, half_rows) + inner


def per_device(
    table_rows,
    item_owner,
    item_row,
    norm_gain,
    router,
    w_gate,
    w_up,
    w_down,
    experts_of,
    grad_mixed,
):
    owners = lax.axis_size("expert")
    z, me = lax.axis_index("dp"), lax.axis_index("expert")
    tokens, levels = item_row.shape
    owner_rows, width = table_rows.shape
    exp_local = w_gate.shape[0]
    top = experts_of.shape[1]
    capacity = 2 * tokens * top // router.shape[1]
    slots = owners * capacity
    cols = width // SIDE
    z_ref = z.reshape(1).astype(I32)

    def exchange(v):
        n = v.shape[1]
        return lax.all_to_all(
            v.reshape(owners, capacity, n), "expert", split_axis=0, concat_axis=0, tiled=True
        ).reshape(slots, n)

    wanted = row_places(item_owner.reshape(tokens, levels), item_row, me, owner_rows)
    steps = (0, 1, -1, 2)
    all_wanted = jnp.concatenate([wanted] + [send_dp(wanted, s) for s in steps[1:]], axis=0)

    strip = lax.dynamic_slice_in_dim(table_rows, z * cols, cols, 1)
    half = owner_rows // 2
    first = jnp.concatenate(ring_pieces(strip[:half], 0, 1), axis=0)
    second = jnp.concatenate(ring_pieces(strip[half:], 1, 0), axis=0)
    pieces = ring_pieces(first, 1, 0) + ring_pieces(second, 0, 1)
    others = [send_sibling(p) for p in pieces]
    place, *sent_grads = route(experts_of, grad_mixed, owners, exp_local, capacity)
    partial = lookup(pieces, all_wanted, 0, tokens)
    found = lookup(others, all_wanted, owners * owner_rows // 2, tokens, partial)
    arrived = [found[0]] + [send_dp(f, -s) for f, s in zip(found[1:], steps[1:])]
    quarters = [arrived[0], arrived[1], arrived[3], arrived[2]]

    sent_rows = dispatch(z_ref, norm_gain.reshape(1, width), place, quarters, exp_local)
    backs, grads = [], None
    for j in range(exp_local):
        ids = jnp.stack([z, me * exp_local + j]).astype(I32)
        x, g = exchange(sent_rows[j]), exchange(sent_grads[j])
        made, *parts = expert(ids, x, g, router, w_gate, w_up, w_down, j)
        backs.append(exchange(made))
        add = lambda a, b: (a.astype(F32) + b.astype(F32)).astype(BF16)
        far_low, far_high = send_dp(parts[4], 1), send_dp(parts[5], -1)
        before = [None, send_dp(parts[3], 1)]
        after = [send_dp(parts[6], -1), None]
        before[0] = send_dp(add(parts[2], far_low), 1)
        after[1] = send_dp(add(parts[7], far_high), -1)
        grads = finish(parts[0:2], before, after, j, exp_local, grads)
    mixed = combine(z_ref, place, quarters, backs)
    return (mixed, *grads)


def solution(mesh):
    placed = (
        P("expert", None),
        P(("dp", "expert"), None, None),
        P(("dp", "expert"), None),
        P(),
        P(),
        P("expert", None, None),
        P("expert", None, None),
        P("expert", None, None),
        P(("dp", "expert"), None),
        P(("dp", "expert"), None),
    )
    return jax.shard_map(
        per_device,
        mesh=mesh,
        in_specs=placed,
        out_specs=(
            P(("dp", "expert"), None),
            P("expert", "dp", None),
            P("expert", "dp", None),
            P("expert", "dp", None),
        ),
        check_vma=False,
    )
```

```python
import functools

import jax
import jax.numpy as jnp
from jax import lax
from jax.experimental import pallas as pl
from jax.experimental.pallas import tpu as pltpu
from jax.sharding import PartitionSpec as P

BF16, F32, I32 = jnp.bfloat16, jnp.float32, jnp.int32
SIDE = 4
VMEM_BYTES = 56 * 1024 * 1024
PARAMS = pltpu.CompilerParams(vmem_limit_bytes=VMEM_BYTES)
WHOLE = pl.BlockSpec(memory_space=pltpu.VMEM)
SCALAR = pl.BlockSpec(memory_space=pltpu.SMEM)


def cost(flops, nbytes):
    return pl.CostEstimate(flops=int(flops), bytes_accessed=int(nbytes), transcendentals=0)


def dot(a, b):
    return lax.dot_general(a, b, (((1,), (0,)), ((), ())), preferred_element_type=F32)


def dot_t0(a, b):
    return lax.dot_general(a, b, (((0,), (0,)), ((), ())), preferred_element_type=F32)


def dot_t1(a, b):
    return lax.dot_general(a, b, (((1,), (1,)), ((), ())), preferred_element_type=F32)


def after(value, *done):
    return lax.optimization_barrier((value, *done))[0]


def plane_perm(dy, dx, swap=0):
    pairs = []
    for y in range(SIDE):
        for x in range(SIDE):
            for c in range(2):
                to = ((y + dy) % SIDE) * SIDE + (x + dx) % SIDE
                pairs.append(((y * SIDE + x) * 2 + c, to * 2 + (c ^ swap)))
    return pairs


def send_plane(v, dy, dx):
    return lax.ppermute(v, "expert", plane_perm(dy, dx))


def send_sibling(v):
    return lax.ppermute(v, "expert", plane_perm(0, 0, 1))


def send_dp(v, step):
    return lax.ppermute(v, "dp", [(i, (i + step) % SIDE) for i in range(SIDE)])


def ring_pieces(a, dy, dx):
    half = a.shape[0] // 2
    before = send_plane(a, dy, dx)
    after = send_plane(a, -dy, -dx)
    opposite_low = send_plane(before[:half], dy, dx)
    opposite_high = send_plane(after[half:], -dy, -dx)
    return [a, before, after, opposite_low, opposite_high]


def route_kernel(exp_local, capacity, experts_ref, place_ref, partner_ref):
    tokens, top = experts_ref.shape
    owners_slots = place_ref.shape[1] // exp_local
    lanes = partner_ref.shape[1]
    chosen = experts_ref[...]
    ids = lax.broadcasted_iota(I32, (tokens, lanes), 1)
    picks = [(chosen[:, k : k + 1] == ids).astype(F32) for k in range(top)]
    earlier = (
        lax.broadcasted_iota(I32, (tokens, tokens), 0)
        > lax.broadcasted_iota(I32, (tokens, tokens), 1)
    ).astype(F32).astype(BF16)
    slots = lax.broadcasted_iota(I32, (tokens, place_ref.shape[1]), 1)
    total = jnp.zeros((1, lanes), F32)
    hits = []
    for k in range(top):
        ahead = dot(earlier, picks[k].astype(BF16)) + total
        total = total + jnp.sum(picks[k], axis=0, keepdims=True)
        position = jnp.sum(ahead * picks[k], axis=1, keepdims=True).astype(I32)
        expert = chosen[:, k : k + 1]
        column = (
            lax.rem(expert, exp_local) * owners_slots
            + lax.div(expert, exp_local) * capacity
            + position
        )
        hits.append((slots == column).astype(F32))
    place_ref[...] = (hits[0] + hits[1]).astype(BF16)
    partner = dot_t0(hits[0].astype(BF16), picks[1].astype(BF16))
    partner = partner + dot_t0(hits[1].astype(BF16), picks[0].astype(BF16))
    partner_ref[...] = partner.astype(BF16)


def route(experts_of, owners, exp_local, capacity):
    tokens = experts_of.shape[0]
    slots = exp_local * owners * capacity
    return pl.pallas_call(
        functools.partial(route_kernel, exp_local, capacity),
        out_shape=[
            jax.ShapeDtypeStruct((tokens, slots), BF16),
            jax.ShapeDtypeStruct((slots, 128), BF16),
        ],
        in_specs=[WHOLE],
        out_specs=[WHOLE, WHOLE],
        compiler_params=PARAMS,
        cost_estimate=cost(8 * tokens * slots * 128, 1e6),
        name="route",
    )(experts_of)


def lookup_kernel(count, first, has_partial, *refs):
    pieces, rows_ref = refs[:count], refs[count]
    rest = refs[count + 1 :]
    wanted = rows_ref[...]
    levels = wanted.shape[1]
    rows = [wanted[:, i : i + 1] for i in range(levels)]
    named = [(rows[i], sum((r == rows[i]).astype(F32) for r in rows[i:])) for i in range(levels)]
    if has_partial:
        total = rest[0][...]
        rest = rest[1:]
    else:
        total = jnp.zeros((wanted.shape[0], pieces[0].shape[1]), F32)
    at = first
    for piece in pieces:
        span = piece.shape[0]
        ids = lax.broadcasted_iota(I32, (wanted.shape[0], span), 1) + at
        many = jnp.zeros((wanted.shape[0], span), F32)
        for row, times in reversed(named):
            many = jnp.where(row == ids, times, many)
        total = total + dot(many.astype(BF16), piece[...])
        at += span
    if has_partial:
        block = pl.program_id(0)
        for i, out in enumerate(rest):

            @pl.when(block == i)
            def _():
                out[...] = total.astype(BF16)
    else:
        rest[0][...] = total


def lookup(pieces, rows, first, tok, partial=None):
    width = pieces[0].shape[1]
    tokens, levels = rows.shape
    blocks = tokens // tok
    held = sum(p.shape[0] for p in pieces)
    in_specs = [pl.BlockSpec(p.shape, lambda i: (0, 0)) for p in pieces]
    in_specs.append(pl.BlockSpec((tok, levels), lambda i: (i, 0)))
    args = list(pieces) + [rows]
    if partial is None:
        out_shape = jax.ShapeDtypeStruct((tokens, width), F32)
        out_specs = pl.BlockSpec((tok, width), lambda i: (i, 0))
    else:
        in_specs.append(pl.BlockSpec((tok, width), lambda i: (i, 0)))
        args.append(partial)
        out_shape = [jax.ShapeDtypeStruct((tok, width), BF16)] * blocks
        out_specs = [pl.BlockSpec((tok, width), lambda i: (0, 0))] * blocks
    return pl.pallas_call(
        functools.partial(lookup_kernel, len(pieces), first, partial is not None),
        grid=(blocks,),
        out_shape=out_shape,
        in_specs=in_specs,
        out_specs=out_specs,
        compiler_params=PARAMS,
        cost_estimate=cost(2 * tokens * held * width, held * width * 2 + tokens * width * 4),
        name="lookup",
    )(*args)


def dispatch_kernel(with_rows, with_grads, z_ref, gain_ref, place_ref, partner_ref, grad_ref, *refs):
    quarters, out = refs[:-1], refs[-1]
    width = gain_ref.shape[1]
    cols = width // SIDE
    place = place_ref[...]
    if with_rows:
        base = [q[...].astype(F32) for q in quarters]
        total = sum(jnp.sum(b * b, axis=1, keepdims=True) for b in base)
        scale = lax.rsqrt(total / width + 1e-05)
        for r in range(SIDE):
            at = pl.multiple_of(lax.rem(z_ref[0] + r, SIDE) * cols, cols)
            normed = (base[r] * scale * gain_ref[:, pl.ds(at, cols)]).astype(BF16)
            out[:, pl.ds(at, cols)] = dot_t0(place, normed).astype(BF16)
    if with_grads:
        first = width if with_rows else 0
        for at in range(0, width, cols):
            rows = dot_t0(place, grad_ref[:, at : at + cols]).astype(BF16)
            out[:, first + at : first + at + cols] = rows
        out[:, first + width :] = partner_ref[...]


def dispatch(z, gain, place, partner, grads, quarters, j, exp_local, with_grads):
    tokens, width = grads.shape
    slots = place.shape[1] // exp_local
    wide = (width if quarters else 0) + (width + 128 if with_grads else 0)
    whole = lambda a: pl.BlockSpec(a.shape, lambda i: (0, 0))
    return pl.pallas_call(
        functools.partial(dispatch_kernel, bool(quarters), with_grads),
        grid=(1,),
        out_shape=jax.ShapeDtypeStruct((slots, wide), BF16),
        in_specs=[
            SCALAR,
            whole(gain),
            pl.BlockSpec((tokens, slots), lambda i: (0, j)),
            pl.BlockSpec((slots, 128), lambda i: (j, 0)),
            whole(grads) if with_grads else pl.BlockSpec(memory_space=pl.ANY),
        ]
        + [whole(q) for q in quarters],
        out_specs=pl.BlockSpec((slots, wide), lambda i: (0, 0)),
        compiler_params=PARAMS,
        cost_estimate=cost(2 * tokens * slots * wide, 6e6),
        name="dispatch",
    )(z, gain, place, partner, grads, *quarters)


def expert_kernel(count_rows, ids_ref, *refs):
    rows_refs, (router_ref, wg_ref, wu_ref, wd_ref, *refs) = refs[:count_rows], refs[count_rows:]
    out_ref, refs = refs[-10], refs[-9:]
    mine, plus, plus_next, minus, minus_next, weight_ref, xt_ref, gt_ref, acc_ref = refs
    step = pl.program_id(0)
    slots, width = rows_refs[0].shape[0], wg_ref.shape[1]
    first = width if count_rows == 1 else 0
    x_ref, g_ref = rows_refs[0].at[:, :width], rows_refs[-1].at[:, first : first + width]
    quarter = width // SIDE
    half = quarter // 2

    @pl.when(step == 0)
    def _():
        score = jax.nn.sigmoid(dot(x_ref[...], router_ref[...]))
        count = score.shape[1]
        lane = lax.broadcasted_iota(I32, score.shape, 1)
        own = jnp.sum(jnp.where(lane == ids_ref[1], score, 0.0), axis=1, keepdims=True)
        partner = rows_refs[-1][:, first + width : first + width + count].astype(F32)
        other = jnp.sum(score * partner, axis=1, keepdims=True)
        weight_ref[...] = own / (own + other)
        for at in range(0, width, quarter):
            xt_ref[at : at + quarter, :] = x_ref[:, at : at + quarter].T
            gt_ref[at : at + quarter, :] = g_ref[:, at : at + quarter].T
        acc_ref[...] = jnp.zeros_like(acc_ref)

    weight = weight_ref[...]
    gate = dot(x_ref[...], wg_ref[0])
    up = dot(x_ref[...], wu_ref[0])
    grad_hidden = dot(g_ref[...], wd_ref[0]) * weight
    sig = jax.nn.sigmoid(gate)
    act = gate * sig
    hidden = (act * up * weight).astype(BF16)
    grad_gate = (grad_hidden * up * sig * (1.0 + gate * (1.0 - sig))).astype(BF16)
    grad_up = (grad_hidden * act).astype(BF16)
    acc_ref[...] += dot_t1(hidden, wd_ref[0])
    for r, h, part, at in (
        (0, 0, mine, 0),
        (0, 1, mine, half),
        (2, 0, plus, 0),
        (1, 1, plus, half),
        (1, 0, plus_next, 0),
        (2, 1, minus, 0),
        (3, 0, minus, half),
        (3, 1, minus_next, 0),
    ):
        start = lax.rem(ids_ref[0] + r, SIDE) * quarter + h * half
        rows = pl.ds(pl.multiple_of(start, half), half)
        part[0, at : at + half] = dot(xt_ref[rows, :], grad_gate).astype(BF16)
        part[1, at : at + half] = dot(xt_ref[rows, :], grad_up).astype(BF16)
        part[2, at : at + half] = dot(gt_ref[rows, :], hidden).astype(BF16)

    @pl.when(step == pl.num_programs(0) - 1)
    def _():
        out_ref[...] = acc_ref[...].astype(BF16).reshape(out_ref.shape)


def expert(ids, rows, router, w_gate, w_up, w_down, j, made, capacity):
    slots, (_, width, ff) = rows[0].shape[0], w_gate.shape
    chunk = 256 if ff % 256 == 0 else ff
    eighth = width // SIDE // 2
    held = pl.BlockSpec((1, width, chunk), lambda f, ids: (j, 0, f))
    fixed = lambda a: pl.BlockSpec(a.shape, lambda f, ids: (0, 0))
    heights = [2 * eighth, 2 * eighth, eighth, 2 * eighth, eighth]
    grid_spec = pltpu.PrefetchScalarGridSpec(
        num_scalar_prefetch=1,
        grid=(ff // chunk,),
        in_specs=[
            *[fixed(r) for r in rows],
            fixed(router),
            held,
            held,
            held,
        ]
        + [pl.BlockSpec(memory_space=pl.ANY)] * (made is not None),
        out_specs=[pl.BlockSpec((slots // capacity, 1, capacity, width), lambda f, ids: (0, j, 0, 0))]
        + [pl.BlockSpec((3, h, chunk), lambda f, ids: (0, 0, f)) for h in heights],
        scratch_shapes=[
            pltpu.VMEM((slots, 1), F32),
            pltpu.VMEM((width, slots), BF16),
            pltpu.VMEM((width, slots), BF16),
            pltpu.VMEM((slots, width), F32),
        ],
    )
    return pl.pallas_call(
        functools.partial(expert_kernel, len(rows)),
        grid_spec=grid_spec,
        out_shape=[jax.ShapeDtypeStruct((slots // capacity, w_gate.shape[0], capacity, width), BF16)]
        + [jax.ShapeDtypeStruct((3, h, ff), BF16) for h in heights],
        input_output_aliases={} if made is None else {5 + len(rows): 0},
        compiler_params=PARAMS,
        cost_estimate=cost(14 * slots * width * ff, 12 * width * ff + 6 * slots * width),
        name="expert",
    )(ids, *rows, router, w_gate, w_up, w_down, *([] if made is None else [made]))


def finish_kernel(mine, near_high, near_low, last_low, last_high, *refs):
    outs = refs[-3:]
    half = last_low.shape[1]
    for i, out in enumerate(outs):
        low, high = mine[i, :half].astype(F32), mine[i, half:].astype(F32)
        low = low + near_low[i].astype(F32) + last_low[i].astype(F32)
        high = high + near_high[i].astype(F32) + last_high[i].astype(F32)
        out[0, :half, :] = low.astype(BF16)
        out[0, half:, :] = high.astype(BF16)


def finish(mine, plus, minus, last_low, last_high, j, exp_local, held=None):
    _, half, ff = last_low.shape
    chunk = 256 if ff % 256 == 0 else ff
    block = pl.BlockSpec((3, half, chunk), lambda f: (0, 0, f))
    second = pl.BlockSpec((3, half, chunk), lambda f: (0, 1, f))
    in_specs = [pl.BlockSpec((3, 2 * half, chunk), lambda f: (0, 0, f)), second, second, block, block]
    args = [mine, plus, minus, last_low, last_high]
    alias = {}
    if held is not None:
        in_specs += [pl.BlockSpec(memory_space=pl.ANY)] * 3
        args += list(held)
        alias = {5: 0, 6: 1, 7: 2}
    return pl.pallas_call(
        finish_kernel,
        grid=(ff // chunk,),
        out_shape=[jax.ShapeDtypeStruct((exp_local, 2 * half, ff), BF16)] * 3,
        in_specs=in_specs,
        out_specs=[pl.BlockSpec((1, 2 * half, chunk), lambda f: (j, 0, f))] * 3,
        input_output_aliases=alias,
        compiler_params=PARAMS,
        cost_estimate=cost(6 * half * ff * 3, 48 * half * ff),
        name="finish",
    )(*args)


def combine_kernel(z_ref, place_ref, *refs):
    quarters, back, out = refs[:SIDE], refs[SIDE], refs[-1]
    cols = quarters[0].shape[1]
    slots = back.shape[0] * back.shape[2]
    for r in range(SIDE):
        at = pl.multiple_of(lax.rem(z_ref[0] + r, SIDE) * cols, cols)
        total = quarters[r][...].astype(F32)
        for j in range(back.shape[1]):
            rows = back[:, j, :, pl.ds(at, cols)].reshape(slots, cols)
            total = total + dot(place_ref[:, j * slots : (j + 1) * slots], rows)
        out[:, pl.ds(at, cols)] = total.astype(BF16)


def combine(z, place, quarters, back):
    tokens, cols = quarters[0].shape
    return pl.pallas_call(
        combine_kernel,
        out_shape=jax.ShapeDtypeStruct((tokens, SIDE * cols), BF16),
        in_specs=[SCALAR] + [WHOLE] * (2 + SIDE),
        out_specs=WHOLE,
        compiler_params=PARAMS,
        cost_estimate=cost(2 * tokens * place.shape[1] * cols * SIDE, 7e6),
        name="combine",
    )(z, place, *quarters, back)


def row_places(owner, row, me, owner_rows):
    chip, core = owner // 2, owner % 2
    order = lambda d: jnp.where(d == 0, 0, jnp.where(d == 1, 2, jnp.where(d == 2, 3, 1)))
    dy = order((chip // SIDE - me // (2 * SIDE)) % SIDE)
    dx = order((chip % SIDE - (me // 2) % SIDE) % SIDE)
    half = owner_rows // 2
    inner = jnp.where(row < half, dy * SIDE + dx, dx * SIDE + dy) * half + row % half
    half_rows = SIDE * SIDE * half
    other = (core != me % 2).astype(I32)
    return other * (2 * half_rows) + jnp.where(row < half, 0, half_rows) + inner


def per_device(
    table_rows,
    item_owner,
    item_row,
    norm_gain,
    router,
    w_gate,
    w_up,
    w_down,
    experts_of,
    grad_mixed,
):
    owners = lax.axis_size("expert")
    z, me = lax.axis_index("dp"), lax.axis_index("expert")
    tokens, levels = item_row.shape
    owner_rows, width = table_rows.shape
    exp_local = w_gate.shape[0]
    top = experts_of.shape[1]
    capacity = 2 * tokens * top // router.shape[1]
    slots = owners * capacity
    cols = width // SIDE
    z_ref = z.reshape(1).astype(I32)

    def exchange(v):
        n = v.shape[1]
        return lax.all_to_all(
            v.reshape(owners, capacity, n), "expert", split_axis=0, concat_axis=0, tiled=True
        ).reshape(slots, n)

    wanted = row_places(item_owner.reshape(tokens, levels), item_row, me, owner_rows)
    steps = (0, 1, -1, 2)
    strip = lax.dynamic_slice_in_dim(table_rows, z * cols, cols, 1)
    half = owner_rows // 2
    along_x, along_y = ring_pieces(strip[:half], 0, 1), ring_pieces(strip[half:], 1, 0)
    place, partner = route(after(experts_of, along_x[1]), owners, exp_local, capacity)
    first = jnp.concatenate(along_x, axis=0)
    second = jnp.concatenate(along_y, axis=0)
    pieces = ring_pieces(first, 1, 0) + ring_pieces(second, 0, 1)
    wishes = after(wanted, first, second)
    asked = jnp.concatenate([send_dp(wishes, s) for s in steps[1:]], axis=0)
    others = [send_sibling(p) for p in pieces]
    gain = norm_gain.reshape(1, width)
    sent = dispatch(z_ref, gain, place, partner, grad_mixed, [], 0, exp_local, True)
    early = exchange(after(sent, asked, pieces[3], pieces[4], pieces[8], pieces[9]))
    partial = lookup(pieces, asked, 0, tokens)
    found = lookup(others, asked, owners * owner_rows // 2, tokens, partial)
    [own] = lookup(pieces + others, wanted, 0, tokens, jnp.zeros((tokens, cols), F32))
    arrived = [own] + [send_dp(f, -s) for f, s in zip(found, steps[1:])]
    quarters = [arrived[0], arrived[1], arrived[3], arrived[2]]

    add = lambda a, b: (a.astype(F32) + b.astype(F32)).astype(BF16)
    made, waves = None, []
    for j in range(exp_local):
        ids = jnp.stack([z, me * exp_local + j]).astype(I32)
        sent = dispatch(z_ref, gain, place, partner, grad_mixed, quarters, j, exp_local, j > 0)
        rows = [exchange(sent)] + [early] * (j == 0)
        made, mine, plus, plus_next, minus, minus_next = expert(
            ids, rows, router, w_gate, w_up, w_down, j, made, capacity
        )
        waves.append((mine, send_dp(plus, 1), send_dp(minus, -1), plus_next, minus_next))
    eighth = width // SIDE // 2
    for j, (mine, plus, minus, plus_next, minus_next) in enumerate(waves):
        plus, minus = after((plus, minus), made)
        low, high = add(plus_next, plus[:, :eighth]), add(minus_next, minus[:, :eighth])
        waves[j] = (mine, plus, minus, send_dp(low, 1), send_dp(high, -1))
    back = lax.all_to_all(made, "expert", split_axis=0, concat_axis=0, tiled=True)
    mixed = combine(z_ref, place, quarters, back)
    grads = None
    for j, wave in enumerate(waves):
        if j == exp_local - 1:
            wave = after(wave, mixed)
        grads = finish(*wave, j, exp_local, grads)
    return (mixed, *grads)


def solution(mesh):
    placed = (
        P("expert", None),
        P(("dp", "expert"), None, None),
        P(("dp", "expert"), None),
        P(),
        P(),
        P("expert", None, None),
        P("expert", None, None),
        P("expert", None, None),
        P(("dp", "expert"), None),
        P(("dp", "expert"), None),
    )
    return jax.shard_map(
        per_device,
        mesh=mesh,
        in_specs=placed,
        out_specs=(
            P(("dp", "expert"), None),
            P("expert", "dp", None),
            P("expert", "dp", None),
            P("expert", "dp", None),
        ),
        check_vma=False,
    )
```

```python
import functools

import jax
import jax.numpy as jnp
from jax import lax
from jax.experimental import pallas as pl
from jax.experimental.pallas import tpu as pltpu
from jax.sharding import PartitionSpec as P

BF16, F32, I32 = jnp.bfloat16, jnp.float32, jnp.int32
SIDE = 4
VMEM_BYTES = 56 * 1024 * 1024
PARAMS = pltpu.CompilerParams(vmem_limit_bytes=VMEM_BYTES)
WHOLE = pl.BlockSpec(memory_space=pltpu.VMEM)
SCALAR = pl.BlockSpec(memory_space=pltpu.SMEM)


def cost(flops, nbytes):
    return pl.CostEstimate(flops=int(flops), bytes_accessed=int(nbytes), transcendentals=0)


def dot(a, b):
    return lax.dot_general(a, b, (((1,), (0,)), ((), ())), preferred_element_type=F32)


def dot_t0(a, b):
    return lax.dot_general(a, b, (((0,), (0,)), ((), ())), preferred_element_type=F32)


def dot_t1(a, b):
    return lax.dot_general(a, b, (((1,), (1,)), ((), ())), preferred_element_type=F32)


def after(value, *done):
    return lax.optimization_barrier((value, *done))[0]


def plane_perm(dy, dx, swap=0):
    pairs = []
    for y in range(SIDE):
        for x in range(SIDE):
            for c in range(2):
                to = ((y + dy) % SIDE) * SIDE + (x + dx) % SIDE
                pairs.append(((y * SIDE + x) * 2 + c, to * 2 + (c ^ swap)))
    return pairs


def send_plane(v, dy, dx):
    return lax.ppermute(v, "expert", plane_perm(dy, dx))


def send_sibling(v):
    return lax.ppermute(v, "expert", plane_perm(0, 0, 1))


def send_dp(v, step):
    return lax.ppermute(v, "dp", [(i, (i + step) % SIDE) for i in range(SIDE)])


def ring_pieces(a, dy, dx):
    half = a.shape[0] // 2
    before = send_plane(a, dy, dx)
    after = send_plane(a, -dy, -dx)
    opposite_low = send_plane(before[:half], dy, dx)
    opposite_high = send_plane(after[half:], -dy, -dx)
    return [a, before, after, opposite_low, opposite_high]


def route_kernel(exp_local, capacity, experts_ref, place_ref, partner_ref):
    tokens, top = experts_ref.shape
    owners_slots = place_ref.shape[1] // exp_local
    lanes = partner_ref.shape[1]
    chosen = experts_ref[...]
    ids = lax.broadcasted_iota(I32, (tokens, lanes), 1)
    picks = [(chosen[:, k : k + 1] == ids).astype(F32) for k in range(top)]
    earlier = (
        lax.broadcasted_iota(I32, (tokens, tokens), 0)
        > lax.broadcasted_iota(I32, (tokens, tokens), 1)
    ).astype(F32).astype(BF16)
    slots = lax.broadcasted_iota(I32, (tokens, place_ref.shape[1]), 1)
    total = jnp.zeros((1, lanes), F32)
    hits = []
    for k in range(top):
        ahead = dot(earlier, picks[k].astype(BF16)) + total
        total = total + jnp.sum(picks[k], axis=0, keepdims=True)
        position = jnp.sum(ahead * picks[k], axis=1, keepdims=True).astype(I32)
        expert = chosen[:, k : k + 1]
        column = (
            lax.rem(expert, exp_local) * owners_slots
            + lax.div(expert, exp_local) * capacity
            + position
        )
        hits.append((slots == column).astype(F32))
    place_ref[...] = (hits[0] + hits[1]).astype(BF16)
    partner = dot_t0(hits[0].astype(BF16), picks[1].astype(BF16))
    partner = partner + dot_t0(hits[1].astype(BF16), picks[0].astype(BF16))
    partner_ref[...] = partner.astype(BF16)


def route(experts_of, owners, exp_local, capacity):
    tokens = experts_of.shape[0]
    slots = exp_local * owners * capacity
    return pl.pallas_call(
        functools.partial(route_kernel, exp_local, capacity),
        out_shape=[
            jax.ShapeDtypeStruct((tokens, slots), BF16),
            jax.ShapeDtypeStruct((slots, 128), BF16),
        ],
        in_specs=[WHOLE],
        out_specs=[WHOLE, WHOLE],
        compiler_params=PARAMS,
        cost_estimate=cost(8 * tokens * slots * 128, 1e6),
        name="route",
    )(experts_of)


def lookup_kernel(count, first, has_partial, last, *refs):
    pieces, rows_ref = refs[:count], refs[count]
    rest = refs[count + 1 :]
    wanted = rows_ref[...]
    levels = wanted.shape[1]
    rows = [wanted[:, i : i + 1] for i in range(levels)]
    named = [(rows[i], sum((r == rows[i]).astype(F32) for r in rows[i:])) for i in range(levels)]
    if has_partial:
        total = rest[0][...]
        rest = rest[1:]
    else:
        total = jnp.zeros((wanted.shape[0], pieces[0].shape[1]), F32)
    at = first
    for piece in pieces:
        span = piece.shape[0]
        ids = lax.broadcasted_iota(I32, (wanted.shape[0], span), 1) + at
        many = jnp.zeros((wanted.shape[0], span), F32)
        for row, times in reversed(named):
            many = jnp.where(row == ids, times, many)
        total = total + dot(many.astype(BF16), piece[...])
        at += span
    if last:
        block = pl.program_id(0)
        for i, out in enumerate(rest):

            @pl.when(block == i)
            def _():
                out[...] = total.astype(BF16)
    else:
        rest[0][...] = total


def lookup(pieces, rows, first, tok, partial=None, last=True):
    width = pieces[0].shape[1]
    tokens, levels = rows.shape
    blocks = tokens // tok
    held = sum(p.shape[0] for p in pieces)
    in_specs = [pl.BlockSpec(p.shape, lambda i: (0, 0)) for p in pieces]
    in_specs.append(pl.BlockSpec((tok, levels), lambda i: (i, 0)))
    args = list(pieces) + [rows]
    if partial is not None:
        in_specs.append(pl.BlockSpec((tok, width), lambda i: (i, 0)))
        args.append(partial)
    if not last:
        out_shape = jax.ShapeDtypeStruct((tokens, width), F32)
        out_specs = pl.BlockSpec((tok, width), lambda i: (i, 0))
    else:
        out_shape = [jax.ShapeDtypeStruct((tok, width), BF16)] * blocks
        out_specs = [pl.BlockSpec((tok, width), lambda i: (0, 0))] * blocks
    return pl.pallas_call(
        functools.partial(lookup_kernel, len(pieces), first, partial is not None, last),
        grid=(blocks,),
        out_shape=out_shape,
        in_specs=in_specs,
        out_specs=out_specs,
        compiler_params=PARAMS,
        cost_estimate=cost(2 * tokens * held * width, held * width * 2 + tokens * width * 4),
        name="lookup",
    )(*args)


def dispatch_kernel(with_rows, with_grads, z_ref, gain_ref, place_ref, partner_ref, grad_ref, *refs):
    quarters, out = refs[:-1], refs[-1]
    width = gain_ref.shape[1]
    cols = width // SIDE
    place = place_ref[...]
    if with_rows:
        base = [q[...].astype(F32) for q in quarters]
        total = sum(jnp.sum(b * b, axis=1, keepdims=True) for b in base)
        scale = lax.rsqrt(total / width + 1e-05)
        for r in range(SIDE):
            at = pl.multiple_of(lax.rem(z_ref[0] + r, SIDE) * cols, cols)
            normed = (base[r] * scale * gain_ref[:, pl.ds(at, cols)]).astype(BF16)
            out[:, pl.ds(at, cols)] = dot_t0(place, normed).astype(BF16)
    if with_grads:
        first = width if with_rows else 0
        for at in range(0, width, cols):
            rows = dot_t0(place, grad_ref[:, at : at + cols]).astype(BF16)
            out[:, first + at : first + at + cols] = rows
        out[:, first + width :] = partner_ref[...]


def dispatch(z, gain, place, partner, grads, quarters, j, exp_local, with_grads):
    tokens, width = grads.shape
    slots = place.shape[1] // exp_local
    wide = (width if quarters else 0) + (width + 128 if with_grads else 0)
    whole = lambda a: pl.BlockSpec(a.shape, lambda i: (0, 0))
    return pl.pallas_call(
        functools.partial(dispatch_kernel, bool(quarters), with_grads),
        grid=(1,),
        out_shape=jax.ShapeDtypeStruct((slots, wide), BF16),
        in_specs=[
            SCALAR,
            whole(gain),
            pl.BlockSpec((tokens, slots), lambda i: (0, j)),
            pl.BlockSpec((slots, 128), lambda i: (j, 0)),
            whole(grads) if with_grads else pl.BlockSpec(memory_space=pl.ANY),
        ]
        + [whole(q) for q in quarters],
        out_specs=pl.BlockSpec((slots, wide), lambda i: (0, 0)),
        compiler_params=PARAMS,
        cost_estimate=cost(2 * tokens * slots * wide, 6e6),
        name="dispatch",
    )(z, gain, place, partner, grads, *quarters)


def expert_kernel(count_rows, ids_ref, *refs):
    rows_refs, (router_ref, wg_ref, wu_ref, wd_ref, *refs) = refs[:count_rows], refs[count_rows:]
    out_ref, refs = refs[-10], refs[-9:]
    mine, plus, plus_next, minus, minus_next, weight_ref, xt_ref, gt_ref, acc_ref = refs
    step = pl.program_id(0)
    slots, width = rows_refs[0].shape[0], wg_ref.shape[1]
    first = width if count_rows == 1 else 0
    x_ref, g_ref = rows_refs[0].at[:, :width], rows_refs[-1].at[:, first : first + width]
    quarter = width // SIDE
    half = quarter // 2

    @pl.when(step == 0)
    def _():
        score = jax.nn.sigmoid(dot_t1(x_ref[...], router_ref[...]))
        count = score.shape[1]
        lane = lax.broadcasted_iota(I32, score.shape, 1)
        own = jnp.sum(jnp.where(lane == ids_ref[1], score, 0.0), axis=1, keepdims=True)
        partner = rows_refs[-1][:, first + width : first + width + count].astype(F32)
        other = jnp.sum(score * partner, axis=1, keepdims=True)
        weight_ref[...] = own / (own + other)
        for at in range(0, width, quarter):
            xt_ref[at : at + quarter, :] = x_ref[:, at : at + quarter].T
            gt_ref[at : at + quarter, :] = g_ref[:, at : at + quarter].T
        acc_ref[...] = jnp.zeros_like(acc_ref)

    weight = weight_ref[...]
    gate = dot(x_ref[...], wg_ref[0])
    up = dot(x_ref[...], wu_ref[0])
    grad_hidden = dot(g_ref[...], wd_ref[0]) * weight
    sig = jax.nn.sigmoid(gate)
    act = gate * sig
    hidden = (act * up * weight).astype(BF16)
    grad_gate = (grad_hidden * up * sig * (1.0 + gate * (1.0 - sig))).astype(BF16)
    grad_up = (grad_hidden * act).astype(BF16)
    acc_ref[...] += dot_t1(hidden, wd_ref[0])
    for r, h, part, at in (
        (0, 0, mine, 0),
        (0, 1, mine, half),
        (2, 0, plus, 0),
        (1, 1, plus, half),
        (1, 0, plus_next, 0),
        (2, 1, minus, 0),
        (3, 0, minus, half),
        (3, 1, minus_next, 0),
    ):
        start = lax.rem(ids_ref[0] + r, SIDE) * quarter + h * half
        rows = pl.ds(pl.multiple_of(start, half), half)
        part[0, at : at + half] = dot(xt_ref[rows, :], grad_gate).astype(BF16)
        part[1, at : at + half] = dot(xt_ref[rows, :], grad_up).astype(BF16)
        part[2, at : at + half] = dot(gt_ref[rows, :], hidden).astype(BF16)

    @pl.when(step == pl.num_programs(0) - 1)
    def _():
        out_ref[...] = acc_ref[...].astype(BF16).reshape(out_ref.shape)


def expert(ids, rows, router, w_gate, w_up, w_down, j, made, capacity):
    slots, (_, width, ff) = rows[0].shape[0], w_gate.shape
    chunk = 256 if ff % 256 == 0 else ff
    eighth = width // SIDE // 2
    held = pl.BlockSpec((1, width, chunk), lambda f, ids: (j, 0, f))
    fixed = lambda a: pl.BlockSpec(a.shape, lambda f, ids: (0, 0))
    heights = [2 * eighth, 2 * eighth, eighth, 2 * eighth, eighth]
    grid_spec = pltpu.PrefetchScalarGridSpec(
        num_scalar_prefetch=1,
        grid=(ff // chunk,),
        in_specs=[
            *[fixed(r) for r in rows],
            fixed(router),
            held,
            held,
            held,
        ]
        + [pl.BlockSpec(memory_space=pl.ANY)] * (made is not None),
        out_specs=[pl.BlockSpec((slots // capacity, 1, capacity, width), lambda f, ids: (0, j, 0, 0))]
        + [pl.BlockSpec((3, h, chunk), lambda f, ids: (0, 0, f)) for h in heights],
        scratch_shapes=[
            pltpu.VMEM((slots, 1), F32),
            pltpu.VMEM((width, slots), BF16),
            pltpu.VMEM((width, slots), BF16),
            pltpu.VMEM((slots, width), F32),
        ],
    )
    return pl.pallas_call(
        functools.partial(expert_kernel, len(rows)),
        grid_spec=grid_spec,
        out_shape=[jax.ShapeDtypeStruct((slots // capacity, w_gate.shape[0], capacity, width), BF16)]
        + [jax.ShapeDtypeStruct((3, h, ff), BF16) for h in heights],
        input_output_aliases={} if made is None else {5 + len(rows): 0},
        compiler_params=PARAMS,
        cost_estimate=cost(14 * slots * width * ff, 12 * width * ff + 6 * slots * width),
        name="expert",
    )(ids, *rows, router, w_gate, w_up, w_down, *([] if made is None else [made]))


def finish_kernel(mine, near_high, near_low, last_low, last_high, *refs):
    outs = refs[-3:]
    half = last_low.shape[1]
    for i, out in enumerate(outs):
        low, high = mine[i, :half].astype(F32), mine[i, half:].astype(F32)
        low = low + near_low[i].astype(F32) + last_low[i].astype(F32)
        high = high + near_high[i].astype(F32) + last_high[i].astype(F32)
        out[0, :half, :] = low.astype(BF16)
        out[0, half:, :] = high.astype(BF16)


def finish(mine, plus, minus, last_low, last_high, j, exp_local, held=None):
    _, half, ff = last_low.shape
    chunk = 256 if ff % 256 == 0 else ff
    block = pl.BlockSpec((3, half, chunk), lambda f: (0, 0, f))
    second = pl.BlockSpec((3, half, chunk), lambda f: (0, 1, f))
    in_specs = [pl.BlockSpec((3, 2 * half, chunk), lambda f: (0, 0, f)), second, second, block, block]
    args = [mine, plus, minus, last_low, last_high]
    alias = {}
    if held is not None:
        in_specs += [pl.BlockSpec(memory_space=pl.ANY)] * 3
        args += list(held)
        alias = {5: 0, 6: 1, 7: 2}
    return pl.pallas_call(
        finish_kernel,
        grid=(ff // chunk,),
        out_shape=[jax.ShapeDtypeStruct((exp_local, 2 * half, ff), BF16)] * 3,
        in_specs=in_specs,
        out_specs=[pl.BlockSpec((1, 2 * half, chunk), lambda f: (j, 0, f))] * 3,
        input_output_aliases=alias,
        compiler_params=PARAMS,
        cost_estimate=cost(6 * half * ff * 3, 48 * half * ff),
        name="finish",
    )(*args)


def combine_kernel(z_ref, place_ref, *refs):
    quarters, back, out = refs[:SIDE], refs[SIDE], refs[-1]
    cols = quarters[0].shape[1]
    slots = back.shape[0] * back.shape[2]
    for r in range(SIDE):
        at = pl.multiple_of(lax.rem(z_ref[0] + r, SIDE) * cols, cols)
        total = quarters[r][...].astype(F32)
        for j in range(back.shape[1]):
            rows = back[:, j, :, pl.ds(at, cols)].reshape(slots, cols)
            total = total + dot(place_ref[:, j * slots : (j + 1) * slots], rows)
        out[:, pl.ds(at, cols)] = total.astype(BF16)


def combine(z, place, quarters, back):
    tokens, cols = quarters[0].shape
    return pl.pallas_call(
        combine_kernel,
        out_shape=jax.ShapeDtypeStruct((tokens, SIDE * cols), BF16),
        in_specs=[SCALAR] + [WHOLE] * (2 + SIDE),
        out_specs=WHOLE,
        compiler_params=PARAMS,
        cost_estimate=cost(2 * tokens * place.shape[1] * cols * SIDE, 7e6),
        name="combine",
    )(z, place, *quarters, back)


def row_places(owner, row, me, owner_rows):
    chip, core = owner // 2, owner % 2
    order = lambda d: jnp.where(d == 0, 0, jnp.where(d == 1, 2, jnp.where(d == 2, 3, 1)))
    dy = order((chip // SIDE - me // (2 * SIDE)) % SIDE)
    dx = order((chip % SIDE - (me // 2) % SIDE) % SIDE)
    half = owner_rows // 2
    inner = jnp.where(row < half, dy * SIDE + dx, dx * SIDE + dy) * half + row % half
    half_rows = SIDE * SIDE * half
    other = (core != me % 2).astype(I32)
    return other * (2 * half_rows) + jnp.where(row < half, 0, half_rows) + inner


def per_device(
    table_rows,
    item_owner,
    item_row,
    norm_gain,
    router,
    w_gate,
    w_up,
    w_down,
    experts_of,
    grad_mixed,
):
    owners = lax.axis_size("expert")
    z, me = lax.axis_index("dp"), lax.axis_index("expert")
    tokens, levels = item_row.shape
    owner_rows, width = table_rows.shape
    exp_local = w_gate.shape[0]
    top = experts_of.shape[1]
    capacity = 2 * tokens * top // router.shape[1]
    slots = owners * capacity
    cols = width // SIDE
    z_ref = z.reshape(1).astype(I32)

    def exchange(v):
        n = v.shape[1]
        return lax.all_to_all(
            v.reshape(owners, capacity, n), "expert", split_axis=0, concat_axis=0, tiled=True
        ).reshape(slots, n)

    wanted = row_places(item_owner.reshape(tokens, levels), item_row, me, owner_rows)
    steps = (0, 1, -1, 2)
    strip = lax.dynamic_slice_in_dim(table_rows, z * cols, cols, 1)
    half = owner_rows // 2
    along_x, along_y = ring_pieces(strip[:half], 0, 1), ring_pieces(strip[half:], 1, 0)
    place, partner = route(after(experts_of, along_x[1]), owners, exp_local, capacity)
    first = jnp.concatenate(along_x, axis=0)
    second = jnp.concatenate(along_y, axis=0)
    pieces = ring_pieces(first, 1, 0) + ring_pieces(second, 0, 1)
    wishes = after(wanted, first, second)
    asked = jnp.concatenate([send_dp(wishes, s) for s in steps[1:]], axis=0)
    others = [send_sibling(p) for p in pieces]
    gain = norm_gain.reshape(1, width)
    sent = dispatch(z_ref, gain, place, partner, grad_mixed, [], 0, exp_local, True)
    early = exchange(after(sent, asked, pieces[3], pieces[4], pieces[8], pieces[9]))
    partial = lookup(pieces, asked, 0, tokens, last=False)
    found = lookup(others, asked, owners * owner_rows // 2, tokens, partial)
    [own] = lookup(pieces + others, wanted, 0, tokens)
    arrived = [own] + [send_dp(f, -s) for f, s in zip(found, steps[1:])]
    quarters = [arrived[0], arrived[1], arrived[3], arrived[2]]

    add = lambda a, b: (a.astype(F32) + b.astype(F32)).astype(BF16)
    made, waves = None, []
    for j in range(exp_local):
        ids = jnp.stack([z, me * exp_local + j]).astype(I32)
        sent = dispatch(z_ref, gain, place, partner, grad_mixed, quarters, j, exp_local, j > 0)
        rows = [exchange(sent)] + [early] * (j == 0)
        made, mine, plus, plus_next, minus, minus_next = expert(
            ids, rows, router.T, w_gate, w_up, w_down, j, made, capacity
        )
        waves.append((mine, send_dp(plus, 1), send_dp(minus, -1), plus_next, minus_next))
    eighth = width // SIDE // 2
    for j, (mine, plus, minus, plus_next, minus_next) in enumerate(waves):
        plus, minus = after((plus, minus), made)
        low, high = add(plus_next, plus[:, :eighth]), add(minus_next, minus[:, :eighth])
        waves[j] = (mine, plus, minus, send_dp(low, 1), send_dp(high, -1))
    back = lax.all_to_all(made, "expert", split_axis=0, concat_axis=0, tiled=True)
    mixed = combine(z_ref, place, quarters, back)
    grads = None
    for j, wave in enumerate(waves):
        if j == exp_local - 1:
            wave = after(wave, mixed)
        grads = finish(*wave, j, exp_local, grads)
    return (mixed, *grads)


def solution(mesh):
    placed = (
        P("expert", None),
        P(("dp", "expert"), None, None),
        P(("dp", "expert"), None),
        P(),
        P(),
        P("expert", None, None),
        P("expert", None, None),
        P("expert", None, None),
        P(("dp", "expert"), None),
        P(("dp", "expert"), None),
    )
    return jax.shard_map(
        per_device,
        mesh=mesh,
        in_specs=placed,
        out_specs=(
            P(("dp", "expert"), None),
            P("expert", "dp", None),
            P("expert", "dp", None),
            P("expert", "dp", None),
        ),
        check_vma=False,
    )
```

```python
import functools

import jax
import jax.numpy as jnp
from jax import lax
from jax.experimental import pallas as pl
from jax.experimental.pallas import tpu as pltpu
from jax.sharding import PartitionSpec as P

BF16, F32, I32 = jnp.bfloat16, jnp.float32, jnp.int32
SIDE = 4
VMEM_BYTES = 56 * 1024 * 1024
PARAMS = pltpu.CompilerParams(vmem_limit_bytes=VMEM_BYTES)
WHOLE = pl.BlockSpec(memory_space=pltpu.VMEM)
SCALAR = pl.BlockSpec(memory_space=pltpu.SMEM)


def cost(flops, nbytes):
    return pl.CostEstimate(flops=int(flops), bytes_accessed=int(nbytes), transcendentals=0)


def dot(a, b):
    return lax.dot_general(a, b, (((1,), (0,)), ((), ())), preferred_element_type=F32)


def dot_t0(a, b):
    return lax.dot_general(a, b, (((0,), (0,)), ((), ())), preferred_element_type=F32)


def dot_t1(a, b):
    return lax.dot_general(a, b, (((1,), (1,)), ((), ())), preferred_element_type=F32)


def after(value, *done):
    return lax.optimization_barrier((value, *done))[0]


def plane_perm(dy, dx, swap=0):
    pairs = []
    for y in range(SIDE):
        for x in range(SIDE):
            for c in range(2):
                to = ((y + dy) % SIDE) * SIDE + (x + dx) % SIDE
                pairs.append(((y * SIDE + x) * 2 + c, to * 2 + (c ^ swap)))
    return pairs


def send_plane(v, dy, dx):
    return lax.ppermute(v, "expert", plane_perm(dy, dx))


def send_sibling(v):
    return lax.ppermute(v, "expert", plane_perm(0, 0, 1))


def send_dp(v, step):
    return lax.ppermute(v, "dp", [(i, (i + step) % SIDE) for i in range(SIDE)])


def ring_pieces(a, dy, dx):
    half = a.shape[0] // 2
    before = send_plane(a, dy, dx)
    after = send_plane(a, -dy, -dx)
    opposite_low = send_plane(before[:half], dy, dx)
    opposite_high = send_plane(after[half:], -dy, -dx)
    return [a, before, after, opposite_low, opposite_high]


def route_kernel(exp_local, capacity, experts_ref, place_ref, partner_ref):
    tokens, top = experts_ref.shape
    owners_slots = place_ref.shape[1] // exp_local
    lanes = partner_ref.shape[1]
    chosen = experts_ref[...]
    ids = lax.broadcasted_iota(I32, (tokens, lanes), 1)
    picks = [(chosen[:, k : k + 1] == ids).astype(F32) for k in range(top)]
    earlier = (
        lax.broadcasted_iota(I32, (tokens, tokens), 0)
        > lax.broadcasted_iota(I32, (tokens, tokens), 1)
    ).astype(F32).astype(BF16)
    slots = lax.broadcasted_iota(I32, (tokens, place_ref.shape[1]), 1)
    total = jnp.zeros((1, lanes), F32)
    hits = []
    for k in range(top):
        ahead = dot(earlier, picks[k].astype(BF16)) + total
        total = total + jnp.sum(picks[k], axis=0, keepdims=True)
        position = jnp.sum(ahead * picks[k], axis=1, keepdims=True).astype(I32)
        expert = chosen[:, k : k + 1]
        column = (
            lax.rem(expert, exp_local) * owners_slots
            + lax.div(expert, exp_local) * capacity
            + position
        )
        hits.append((slots == column).astype(F32))
    place_ref[...] = (hits[0] + hits[1]).astype(BF16)
    partner = dot_t0(hits[0].astype(BF16), picks[1].astype(BF16))
    partner = partner + dot_t0(hits[1].astype(BF16), picks[0].astype(BF16))
    partner_ref[...] = partner.astype(BF16)


def route(experts_of, owners, exp_local, capacity):
    tokens = experts_of.shape[0]
    slots = exp_local * owners * capacity
    return pl.pallas_call(
        functools.partial(route_kernel, exp_local, capacity),
        out_shape=[
            jax.ShapeDtypeStruct((tokens, slots), BF16),
            jax.ShapeDtypeStruct((slots, 128), BF16),
        ],
        in_specs=[WHOLE],
        out_specs=[WHOLE, WHOLE],
        compiler_params=PARAMS,
        cost_estimate=cost(8 * tokens * slots * 128, 1e6),
        name="route",
    )(experts_of)


def lookup_kernel(count, first, has_partial, last, *refs):
    pieces, rows_ref = refs[:count], refs[count]
    rest = refs[count + 1 :]
    wanted = rows_ref[...]
    levels = wanted.shape[1]
    rows = [wanted[:, i : i + 1] for i in range(levels)]
    named = [(rows[i], sum((r == rows[i]).astype(F32) for r in rows[i:])) for i in range(levels)]
    if has_partial:
        total = rest[0][...]
        rest = rest[1:]
    else:
        total = jnp.zeros((wanted.shape[0], pieces[0].shape[1]), F32)
    at = first
    for piece in pieces:
        span = piece.shape[0]
        ids = lax.broadcasted_iota(I32, (wanted.shape[0], span), 1) + at
        many = jnp.zeros((wanted.shape[0], span), F32)
        for row, times in reversed(named):
            many = jnp.where(row == ids, times, many)
        total = total + dot(many.astype(BF16), piece[...])
        at += span
    if last:
        block = pl.program_id(0)
        for i, out in enumerate(rest):

            @pl.when(block == i)
            def _():
                out[...] = total.astype(BF16)
    else:
        rest[0][...] = total


def lookup(pieces, rows, first, tok, partial=None, last=True):
    width = pieces[0].shape[1]
    tokens, levels = rows.shape
    blocks = tokens // tok
    held = sum(p.shape[0] for p in pieces)
    in_specs = [pl.BlockSpec(p.shape, lambda i: (0, 0)) for p in pieces]
    in_specs.append(pl.BlockSpec((tok, levels), lambda i: (i, 0)))
    args = list(pieces) + [rows]
    if partial is not None:
        in_specs.append(pl.BlockSpec((tok, width), lambda i: (i, 0)))
        args.append(partial)
    if not last:
        out_shape = jax.ShapeDtypeStruct((tokens, width), F32)
        out_specs = pl.BlockSpec((tok, width), lambda i: (i, 0))
    else:
        out_shape = [jax.ShapeDtypeStruct((tok, width), BF16)] * blocks
        out_specs = [pl.BlockSpec((tok, width), lambda i: (0, 0))] * blocks
    return pl.pallas_call(
        functools.partial(lookup_kernel, len(pieces), first, partial is not None, last),
        grid=(blocks,),
        out_shape=out_shape,
        in_specs=in_specs,
        out_specs=out_specs,
        compiler_params=PARAMS,
        cost_estimate=cost(2 * tokens * held * width, held * width * 2 + tokens * width * 4),
        name="lookup",
    )(*args)


def dispatch_kernel(with_rows, with_grads, z_ref, gain_ref, place_ref, partner_ref, grad_ref, *refs):
    quarters, out = refs[:-1], refs[-1]
    width = gain_ref.shape[1]
    cols = width // SIDE
    place = place_ref[...]
    if with_rows:
        base = [q[...].astype(F32) for q in quarters]
        total = sum(jnp.sum(b * b, axis=1, keepdims=True) for b in base)
        scale = lax.rsqrt(total / width + 1e-05)
        for r in range(SIDE):
            at = pl.multiple_of(lax.rem(z_ref[0] + r, SIDE) * cols, cols)
            normed = (base[r] * scale * gain_ref[:, pl.ds(at, cols)]).astype(BF16)
            out[:, pl.ds(at, cols)] = dot_t0(place, normed).astype(BF16)
    if with_grads:
        first = width if with_rows else 0
        for at in range(0, width, cols):
            rows = dot_t0(place, grad_ref[:, at : at + cols]).astype(BF16)
            out[:, first + at : first + at + cols] = rows
        out[:, first + width :] = partner_ref[...]


def dispatch(z, gain, place, partner, grads, quarters, j, exp_local, with_grads):
    tokens, width = grads.shape
    slots = place.shape[1] // exp_local
    wide = (width if quarters else 0) + (width + 128 if with_grads else 0)
    whole = lambda a: pl.BlockSpec(a.shape, lambda i: (0, 0))
    return pl.pallas_call(
        functools.partial(dispatch_kernel, bool(quarters), with_grads),
        grid=(1,),
        out_shape=jax.ShapeDtypeStruct((slots, wide), BF16),
        in_specs=[
            SCALAR,
            whole(gain),
            pl.BlockSpec((tokens, slots), lambda i: (0, j)),
            pl.BlockSpec((slots, 128), lambda i: (j, 0)),
            whole(grads) if with_grads else pl.BlockSpec(memory_space=pl.ANY),
        ]
        + [whole(q) for q in quarters],
        out_specs=pl.BlockSpec((slots, wide), lambda i: (0, 0)),
        compiler_params=PARAMS,
        cost_estimate=cost(2 * tokens * slots * wide, 6e6),
        name="dispatch",
    )(z, gain, place, partner, grads, *quarters)


def expert_kernel(count_rows, ids_ref, *refs):
    rows_refs, (router_ref, wg_ref, wu_ref, wd_ref, *refs) = refs[:count_rows], refs[count_rows:]
    out_ref, refs = refs[-10], refs[-9:]
    mine, plus, plus_next, minus, minus_next, weight_ref, xt_ref, gt_ref, acc_ref = refs
    step = pl.program_id(0)
    slots, width = rows_refs[0].shape[0], wg_ref.shape[1]
    first = width if count_rows == 1 else 0
    x_ref, g_ref = rows_refs[0].at[:, :width], rows_refs[-1].at[:, first : first + width]
    quarter = width // SIDE
    half = quarter // 2

    @pl.when(step == 0)
    def _():
        score = jax.nn.sigmoid(dot_t1(x_ref[...], router_ref[...]))
        count = score.shape[1]
        lane = lax.broadcasted_iota(I32, score.shape, 1)
        own = jnp.sum(jnp.where(lane == ids_ref[1], score, 0.0), axis=1, keepdims=True)
        partner = rows_refs[-1][:, first + width : first + width + count].astype(F32)
        other = jnp.sum(score * partner, axis=1, keepdims=True)
        weight_ref[...] = own / (own + other)
        for at in range(0, width, quarter):
            xt_ref[at : at + quarter, :] = x_ref[:, at : at + quarter].T
            gt_ref[at : at + quarter, :] = g_ref[:, at : at + quarter].T
        acc_ref[...] = jnp.zeros_like(acc_ref)

    weight = weight_ref[...]
    gate = dot(x_ref[...], wg_ref[0])
    up = dot(x_ref[...], wu_ref[0])
    grad_hidden = dot(g_ref[...], wd_ref[0]) * weight
    sig = jax.nn.sigmoid(gate)
    act = gate * sig
    hidden = (act * up * weight).astype(BF16)
    grad_gate = (grad_hidden * up * sig * (1.0 + gate * (1.0 - sig))).astype(BF16)
    grad_up = (grad_hidden * act).astype(BF16)
    acc_ref[...] += dot_t1(hidden, wd_ref[0])
    for r, h, part, at in (
        (0, 0, mine, 0),
        (0, 1, mine, half),
        (2, 0, plus, 0),
        (1, 1, plus, half),
        (1, 0, plus_next, 0),
        (2, 1, minus, 0),
        (3, 0, minus, half),
        (3, 1, minus_next, 0),
    ):
        start = lax.rem(ids_ref[0] + r, SIDE) * quarter + h * half
        rows = pl.ds(pl.multiple_of(start, half), half)
        part[0, at : at + half] = dot(xt_ref[rows, :], grad_gate).astype(BF16)
        part[1, at : at + half] = dot(xt_ref[rows, :], grad_up).astype(BF16)
        part[2, at : at + half] = dot(gt_ref[rows, :], hidden).astype(BF16)

    @pl.when(step == pl.num_programs(0) - 1)
    def _():
        out_ref[...] = acc_ref[...].astype(BF16).reshape(out_ref.shape)


def expert(ids, rows, router, w_gate, w_up, w_down, j, made, capacity):
    slots, (_, width, ff) = rows[0].shape[0], w_gate.shape
    chunk = 256 if ff % 256 == 0 else ff
    eighth = width // SIDE // 2
    held = pl.BlockSpec((1, width, chunk), lambda f, ids: (j, 0, f))
    fixed = lambda a: pl.BlockSpec(a.shape, lambda f, ids: (0, 0))
    heights = [2 * eighth, 2 * eighth, eighth, 2 * eighth, eighth]
    grid_spec = pltpu.PrefetchScalarGridSpec(
        num_scalar_prefetch=1,
        grid=(ff // chunk,),
        in_specs=[
            *[fixed(r) for r in rows],
            fixed(router),
            held,
            held,
            held,
        ]
        + [pl.BlockSpec(memory_space=pl.ANY)] * (made is not None),
        out_specs=[pl.BlockSpec((slots // capacity, 1, capacity, width), lambda f, ids: (0, j, 0, 0))]
        + [pl.BlockSpec((3, h, chunk), lambda f, ids: (0, 0, f)) for h in heights],
        scratch_shapes=[
            pltpu.VMEM((slots, 1), F32),
            pltpu.VMEM((width, slots), BF16),
            pltpu.VMEM((width, slots), BF16),
            pltpu.VMEM((slots, width), F32),
        ],
    )
    return pl.pallas_call(
        functools.partial(expert_kernel, len(rows)),
        grid_spec=grid_spec,
        out_shape=[jax.ShapeDtypeStruct((slots // capacity, w_gate.shape[0], capacity, width), BF16)]
        + [jax.ShapeDtypeStruct((3, h, ff), BF16) for h in heights],
        input_output_aliases={} if made is None else {5 + len(rows): 0},
        compiler_params=PARAMS,
        cost_estimate=cost(14 * slots * width * ff, 12 * width * ff + 6 * slots * width),
        name="expert",
    )(ids, *rows, router, w_gate, w_up, w_down, *([] if made is None else [made]))


def finish_kernel(mine, near_high, near_low, last_low, last_high, *refs):
    outs = refs[-3:]
    half = last_low.shape[1]
    for i, out in enumerate(outs):
        low, high = mine[i, :half].astype(F32), mine[i, half:].astype(F32)
        low = low + near_low[i].astype(F32) + last_low[i].astype(F32)
        high = high + near_high[i].astype(F32) + last_high[i].astype(F32)
        out[0, :half, :] = low.astype(BF16)
        out[0, half:, :] = high.astype(BF16)


def finish(mine, plus, minus, last_low, last_high, j, exp_local, held=None):
    _, half, ff = last_low.shape
    chunk = 384 if ff % 384 == 0 else ff
    block = pl.BlockSpec((3, half, chunk), lambda f: (0, 0, f))
    second = pl.BlockSpec((3, half, chunk), lambda f: (0, 1, f))
    in_specs = [pl.BlockSpec((3, 2 * half, chunk), lambda f: (0, 0, f)), second, second, block, block]
    args = [mine, plus, minus, last_low, last_high]
    alias = {}
    if held is not None:
        in_specs += [pl.BlockSpec(memory_space=pl.ANY)] * 3
        args += list(held)
        alias = {5: 0, 6: 1, 7: 2}
    return pl.pallas_call(
        finish_kernel,
        grid=(ff // chunk,),
        out_shape=[jax.ShapeDtypeStruct((exp_local, 2 * half, ff), BF16)] * 3,
        in_specs=in_specs,
        out_specs=[pl.BlockSpec((1, 2 * half, chunk), lambda f: (j, 0, f))] * 3,
        input_output_aliases=alias,
        compiler_params=PARAMS,
        cost_estimate=cost(6 * half * ff * 3, 48 * half * ff),
        name="finish",
    )(*args)


def combine_kernel(z_ref, place_ref, *refs):
    quarters, back, out = refs[:SIDE], refs[SIDE], refs[-1]
    cols = quarters[0].shape[1]
    slots = back.shape[0] * back.shape[2]
    for r in range(SIDE):
        at = pl.multiple_of(lax.rem(z_ref[0] + r, SIDE) * cols, cols)
        total = quarters[r][...].astype(F32)
        for j in range(back.shape[1]):
            rows = back[:, j, :, pl.ds(at, cols)].reshape(slots, cols)
            total = total + dot(place_ref[:, j * slots : (j + 1) * slots], rows)
        out[:, pl.ds(at, cols)] = total.astype(BF16)


def combine(z, place, quarters, back):
    tokens, cols = quarters[0].shape
    return pl.pallas_call(
        combine_kernel,
        out_shape=jax.ShapeDtypeStruct((tokens, SIDE * cols), BF16),
        in_specs=[SCALAR] + [WHOLE] * (2 + SIDE),
        out_specs=WHOLE,
        compiler_params=PARAMS,
        cost_estimate=cost(2 * tokens * place.shape[1] * cols * SIDE, 7e6),
        name="combine",
    )(z, place, *quarters, back)


def row_places(owner, row, me, owner_rows):
    chip, core = owner // 2, owner % 2
    order = lambda d: jnp.where(d == 0, 0, jnp.where(d == 1, 2, jnp.where(d == 2, 3, 1)))
    dy = order((chip // SIDE - me // (2 * SIDE)) % SIDE)
    dx = order((chip % SIDE - (me // 2) % SIDE) % SIDE)
    half = owner_rows // 2
    inner = jnp.where(row < half, dy * SIDE + dx, dx * SIDE + dy) * half + row % half
    half_rows = SIDE * SIDE * half
    other = (core != me % 2).astype(I32)
    return other * (2 * half_rows) + jnp.where(row < half, 0, half_rows) + inner


def per_device(
    table_rows,
    item_owner,
    item_row,
    norm_gain,
    router,
    w_gate,
    w_up,
    w_down,
    experts_of,
    grad_mixed,
):
    owners = lax.axis_size("expert")
    z, me = lax.axis_index("dp"), lax.axis_index("expert")
    tokens, levels = item_row.shape
    owner_rows, width = table_rows.shape
    exp_local = w_gate.shape[0]
    top = experts_of.shape[1]
    capacity = 2 * tokens * top // router.shape[1]
    slots = owners * capacity
    cols = width // SIDE
    z_ref = z.reshape(1).astype(I32)

    def exchange(v):
        n = v.shape[1]
        return lax.all_to_all(
            v.reshape(owners, capacity, n), "expert", split_axis=0, concat_axis=0, tiled=True
        ).reshape(slots, n)

    wanted = row_places(item_owner.reshape(tokens, levels), item_row, me, owner_rows)
    steps = (0, 1, -1, 2)
    strip = lax.dynamic_slice_in_dim(table_rows, z * cols, cols, 1)
    half = owner_rows // 2
    along_x, along_y = ring_pieces(strip[:half], 0, 1), ring_pieces(strip[half:], 1, 0)
    place, partner = route(after(experts_of, along_x[1]), owners, exp_local, capacity)
    first = jnp.concatenate(along_x, axis=0)
    second = jnp.concatenate(along_y, axis=0)
    pieces = ring_pieces(first, 1, 0) + ring_pieces(second, 0, 1)
    wishes = after(wanted, first, second)
    asked = jnp.concatenate([send_dp(wishes, s) for s in steps[1:]], axis=0)
    others = [send_sibling(p) for p in pieces]
    gain = norm_gain.reshape(1, width)
    sent = dispatch(z_ref, gain, place, partner, grad_mixed, [], 0, exp_local, True)
    early = exchange(after(sent, asked, pieces[3], pieces[4], pieces[8], pieces[9]))
    partial = lookup(pieces, asked, 0, tokens, last=False)
    found = lookup(others, asked, owners * owner_rows // 2, tokens, partial)
    [own] = lookup(pieces + others, wanted, 0, tokens)
    arrived = [own] + [send_dp(f, -s) for f, s in zip(found, steps[1:])]
    quarters = [arrived[0], arrived[1], arrived[3], arrived[2]]

    add = lambda a, b: (a.astype(F32) + b.astype(F32)).astype(BF16)
    made, waves = None, []
    for j in range(exp_local):
        ids = jnp.stack([z, me * exp_local + j]).astype(I32)
        sent = dispatch(z_ref, gain, place, partner, grad_mixed, quarters, j, exp_local, j > 0)
        rows = [exchange(sent)] + [early] * (j == 0)
        made, mine, plus, plus_next, minus, minus_next = expert(
            ids, rows, router.T, w_gate, w_up, w_down, j, made, capacity
        )
        waves.append((mine, send_dp(plus, 1), send_dp(minus, -1), plus_next, minus_next))
    eighth = width // SIDE // 2
    for j, (mine, plus, minus, plus_next, minus_next) in enumerate(waves):
        plus, minus = after((plus, minus), made)
        low, high = add(plus_next, plus[:, :eighth]), add(minus_next, minus[:, :eighth])
        waves[j] = (mine, plus, minus, send_dp(low, 1), send_dp(high, -1))
    back = lax.all_to_all(made, "expert", split_axis=0, concat_axis=0, tiled=True)
    mixed = combine(z_ref, place, quarters, back)
    grads = None
    for j, wave in enumerate(waves):
        if j == exp_local - 1:
            wave = after(wave, mixed)
        grads = finish(*wave, j, exp_local, grads)
    return (mixed, *grads)


def solution(mesh):
    placed = (
        P("expert", None),
        P(("dp", "expert"), None, None),
        P(("dp", "expert"), None),
        P(),
        P(),
        P("expert", None, None),
        P("expert", None, None),
        P("expert", None, None),
        P(("dp", "expert"), None),
        P(("dp", "expert"), None),
    )
    return jax.shard_map(
        per_device,
        mesh=mesh,
        in_specs=placed,
        out_specs=(
            P(("dp", "expert"), None),
            P("expert", "dp", None),
            P("expert", "dp", None),
            P("expert", "dp", None),
        ),
        check_vma=False,
    )
```
